256 devices in a mesh: pool: 16 (over z_hi, y), mp: 16 (over z_lo, x, core).
Axes of the slice: x: 4, y: 4, z: 8 (z_hi: 4, z_lo: 2; z = z_hi * 2 + z_lo), core: 2. Of those that a mesh axis runs over, the one named last changes fastest.
Arguments:
- stored_hidden: bfloat16 [8192, 8192], P('pool', 'mp')
- block_owner: int32 [128], P('pool'), may hold values from 0 to 15, as said below
- block_valid: int32 [128], P('pool'), may hold values from 1 to 64, as said below
- block_start: int32 [128], P('pool'), may hold values from 0 to 16320
- turn_hidden: bfloat16 [8192, 8192], P('pool', 'mp')
- turn_position: int32 [8192], P('pool'), may hold values from 0 to 16895
- kv_weight: bfloat16 [8192, 2048], P(None, 'mp'), may hold values from -0.0625 to 0.0625
- kv_bias: float32 [2048], P('mp'), may hold values from -3 to 3
Outputs:
- restored_cache: bfloat16 [16384, 2048], P('pool', 'mp')
- turn_kv: bfloat16 [8192, 2048], P('pool', 'mp')
The draws below stay inside these ranges and needn't reach their ends.
Inputs may be any that keep to these rules, and one draw needn't show every extreme that they name: `block_owner`: the 8 blocks of one storage shard (blocks s * 8 to s * 8 + 7) have distinct owners; in every draw one owner has a block from every storage shard. `block_valid`: every storage shard has a full block.
All inputs are finite; a program needn't handle non-finite values.
Results may differ from the reference program's by a relative error of at most 0.0012.
Values may be sent and summed in bfloat16 or wider, within the bound.
No kernel may reach another device: no remote copies, remote signals or barrier semaphores. Data moves between devices by JAX's collectives and lax.ppermute only.
A program may use at most 128 MiB of HBM per device.

```python
import jax
import jax.numpy as jnp
from jax import lax

D = 8192
HD = 128
BLK = 64
HMAX = 16384
BLK_DEV = 8
NEW_DEV = 512
KVD = 1024
BLOCKS = 128
STORE_ROWS = 8192
CACHE_ROWS = 16384
TURN_ROWS = 8192
N_POOL = 16


def rough_rows(base, key, rows):
    first, second = jax.random.split(key)
    row_scale = jnp.exp(jax.random.uniform(first, (rows, 1), jnp.float32, 0.0, 2.3026))
    col_scale = jnp.exp(jax.random.uniform(second, (1, D), jnp.float32, -1.2, 1.2))
    return (base * row_scale * col_scale).astype(jnp.bfloat16)


def draw_stored_hidden(key, part):
    key = jax.random.fold_in(key, 11)
    first, second = jax.random.split(key, 2)
    base = jax.random.normal(first, (STORE_ROWS, D), jnp.float32)
    return rough_rows(base, second, STORE_ROWS)


def draw_turn_hidden(key, part):
    key = jax.random.fold_in(key, 23)
    first, second = jax.random.split(key, 2)
    base = jax.random.normal(first, (TURN_ROWS, D), jnp.float32)
    return rough_rows(base, second, TURN_ROWS)


def draw_block_owner(key, part):
    key = jax.random.fold_in(key, 37)
    first, second, third = jax.random.split(key, 3)
    full_group = jax.random.randint(first, (), 0, N_POOL)
    shard_keys = jax.random.split(second, N_POOL)
    scores = jax.vmap(lambda k: jax.random.permutation(k, N_POOL))(shard_keys)
    scores = jnp.where(jnp.arange(N_POOL)[None, :] == full_group, N_POOL, scores)
    chosen = jax.lax.top_k(scores, BLK_DEV)[1]
    order_keys = jax.random.split(third, N_POOL)
    orders = jax.vmap(lambda k: jax.random.permutation(k, BLK_DEV))(order_keys)
    mixed = jnp.take_along_axis(chosen, orders, axis=1)
    return mixed.reshape(BLOCKS).astype(jnp.int32)


def draw_block_valid(key, part):
    key = jax.random.fold_in(key, 41)
    first, second = jax.random.split(key)
    values = jax.random.randint(first, (N_POOL, BLK_DEV), 1, BLK + 1)
    full_index = jax.random.randint(second, (N_POOL, 1), 0, BLK_DEV)
    values = jnp.where(jnp.arange(BLK_DEV)[None, :] == full_index, BLK, values)
    return values.reshape(BLOCKS).astype(jnp.int32)


def place_ends(values, stream_key, least, high):
    extent = values.shape
    place = [jax.random.randint(jax.random.fold_in(stream_key, axis), (), 0, extent[axis]) for axis in range(len(extent))]
    values = values.at[tuple(place)].set(least)
    longest = extent.index(max(extent))
    place[longest] = (place[longest] + 1) % extent[longest]
    return values.at[tuple(place)].set(high)


def steps_of(stream_key, shape, shards, smallest, top_value):
    def one(axis_at, parts):
        draws = jax.random.uniform(jax.random.fold_in(jax.random.fold_in(stream_key, 6), axis_at), (parts,), jnp.float32, smallest / len(shards), top_value / len(shards))
        return jnp.repeat(jnp.exp(draws), shape[axis_at] // parts).reshape((-1,) + (1,) * (len(shape) - axis_at - 1))

    loudness = one(*shards[0])
    for cut in shards[1:]:
        loudness = loudness * one(*cut)
    return loudness


def bell_draw(rng, extent, width, bound, pieces=(), held_as=jnp.bfloat16):
    array = width * jax.random.normal(rng, extent, jnp.float32)
    if pieces:
        array = array * steps_of(rng, extent, pieces, -0.22, 0.18)
    return jnp.clip(array, -bound, bound).astype(held_as)


def setup_inputs(seed: int = 0) -> dict:
    streams_of = jax.random.split(jax.random.key(seed), 9)
    return {
        "stored_hidden": draw_stored_hidden(jax.random.fold_in(streams_of[8], 71), 0),
        "block_owner": draw_block_owner(jax.random.fold_in(streams_of[8], 71), 0),
        "block_valid": draw_block_valid(jax.random.fold_in(streams_of[8], 71), 0),
        "block_start": place_ends(jax.random.randint(streams_of[3], (BLOCKS,), 0, HMAX - BLK + 1), jax.random.fold_in(streams_of[3], 1), 0, HMAX - BLK).astype(jnp.int32),
        "turn_hidden": draw_turn_hidden(jax.random.fold_in(streams_of[8], 71), 0),
        "turn_position": place_ends(jax.random.randint(streams_of[5], (TURN_ROWS,), 0, HMAX + NEW_DEV), jax.random.fold_in(streams_of[5], 1), 0, (HMAX + NEW_DEV) - 1).astype(jnp.int32),
        "kv_weight": bell_draw(streams_of[6], (D, 2 * KVD), D ** -0.5, 0.0625, ((1, 16),)),
        "kv_bias": bell_draw(streams_of[7], (2 * KVD,), 0.5, 3.0, ((0, 16),), jnp.float32),
    }


def project(rows, kv_weight, kv_bias):
    raw = jnp.dot(rows, kv_weight, preferred_element_type=jnp.float32)
    squares = lax.optimization_barrier(jnp.sum(jnp.square(rows.astype(jnp.float32)), axis=1))
    scale = lax.rsqrt(squares / D + 1e-06)
    return raw * scale[:, None] + kv_bias[None, :]

def rotate(values, positions, offset):
    count = values.shape[0]
    heads = values.shape[1] // HD
    shaped = values.reshape(count, heads, HD)
    half = HD // 2
    freq = jnp.exp(-jnp.log(jnp.float32(1000000.0)) * (jnp.arange(half).astype(jnp.float32) * 2.0 / HD))
    angle = positions.astype(jnp.float32)[:, None] * freq[None, :]
    cosine = jnp.cos(angle)[:, None, :]
    sine = jnp.sin(angle)[:, None, :]
    first = shaped[:, :, :half]
    second = shaped[:, :, half:]
    turned = jnp.concatenate([first * cosine - second * sine, second * cosine + first * sine], axis=2)
    is_key = offset + jnp.arange(heads) * HD < KVD
    return jnp.where(is_key[None, :, None], turned, shaped).reshape(count, heads * HD)

def reference(stored_hidden, block_owner, block_valid, block_start, turn_hidden, turn_position, kv_weight, kv_bias):
    offsets = jnp.arange(BLK).astype(jnp.int32)
    blocks = stored_hidden.reshape(BLOCKS, BLK, D)

    def restore_one(items):
        rows, start, valid = items
        pre = project(rows, kv_weight, kv_bias)
        roped = rotate(pre, start + offsets, 0)
        keep = (offsets < valid)[:, None]
        return jnp.where(keep, roped, 0.0).astype(jnp.bfloat16)
    restored = lax.map(restore_one, (blocks, block_start, block_valid))
    owners = block_owner.reshape(N_POOL, BLK_DEV)
    picks = (owners[:, :, None] == jnp.arange(N_POOL)[None, None, :]).astype(jnp.float32)
    shaped = restored.reshape(N_POOL, BLK_DEV, BLK, 2 * KVD).astype(jnp.float32)
    cache = jnp.einsum('sbg,sbrc->gsrc', picks, shaped)
    restored_cache = cache.reshape(CACHE_ROWS, 2 * KVD).astype(jnp.bfloat16)
    turn_pre = project(turn_hidden, kv_weight, kv_bias)
    turn_kv = rotate(turn_pre, turn_position, 0).astype(jnp.bfloat16)
    return (restored_cache, turn_kv)
```

```python
import jax
import jax.numpy as jnp
from jax import lax
from jax.sharding import PartitionSpec as P

D = 8192
HD = 128
BLK = 64
KVD = 1024
NZ = 2
NX = 4
NC = 2
LIFT = 16384.0


def spot(z, x, c):
    return (z * NX + x) * NC + c


def pairs(move):
    return [
        (spot(z, x, c), spot(*move(z, x, c)))
        for z in range(NZ)
        for x in range(NX)
        for c in range(NC)
    ]


def to_z(v):
    return lax.ppermute(v, "mp", pairs(lambda z, x, c: (1 - z, x, c)))


def to_core(v):
    return lax.ppermute(v, "mp", pairs(lambda z, x, c: (z, x, 1 - c)))


def along_x(v, d):
    return lax.ppermute(v, "mp", pairs(lambda z, x, c: (z, (x + d) % NX, c)))


def angles(positions):
    half = HD // 2
    freq = jnp.exp(
        -jnp.log(jnp.float32(1000000.0)) * (jnp.arange(half).astype(jnp.float32) * 2.0 / HD)
    )
    angle = positions.astype(jnp.float32)[:, None] * freq[None, :]
    return jnp.cos(angle), jnp.sin(angle)


def rotate(values, cosine, sine, is_key):
    half = HD // 2
    first = values[:, :half]
    second = values[:, half:]
    turned = jnp.concatenate(
        [first * cosine - second * sine, second * cosine + first * sine], axis=1
    )
    return jnp.where(is_key, turned, values)


def squares_of(rows):
    return jnp.sum(jnp.square(rows.astype(jnp.float32)), axis=1)


def partials(rows, weights):
    outs = []
    for w in weights:
        outs.append(jnp.dot(rows, w, preferred_element_type=jnp.float32))
    return outs


def collect(rows, weights):
    norm = squares_of(rows)
    held = jnp.clip(norm, 1e-36, 1e37)
    down = (LIFT * lax.rsqrt(held))[:, None]
    parts = partials(rows, weights)
    total = norm
    terms = []
    for d in range(1, NX):
        sent = (parts[d] * down).astype(jnp.float16)
        got = along_x(sent, NX - d)
        other = along_x(norm, NX - d)
        total = total + other
        up = jnp.sqrt(jnp.clip(other, 1e-36, 1e37)) * (1.0 / LIFT)
        terms.append((got, up))
    return parts[0], terms, total


def finish(own, terms, total, kv_bias):
    scale = lax.rsqrt(total / D + 1e-06)
    value = own * scale[:, None]
    for got, up in terms:
        value = value + got.astype(jnp.float32) * (up * scale)[:, None]
    return value + kv_bias[None, :]


def shards(
    stored_hidden,
    block_owner,
    block_valid,
    block_start,
    turn_hidden,
    turn_position,
    kv_weight,
    kv_bias,
):
    groups = lax.axis_size("pool")
    me = lax.axis_index("mp")
    x = (me // NC) % NX
    core = me % NC
    z = me // (NC * NX)
    is_key = me * HD < KVD
    local = stored_hidden.shape[1]
    blocks_here = block_owner.shape[0]
    offsets = jnp.arange(BLK)

    by_slab = kv_weight.reshape(NZ, NX, NC * local, HD)

    def slab(d):
        return lax.dynamic_index_in_dim(by_slab, (x + d) % NX, axis=1, keepdims=False)

    def whole(rows):
        near = to_core(rows)
        far = to_z(rows)
        far_near = to_core(far)
        mine = jnp.where(core == 0, jnp.concatenate([rows, near], 1), jnp.concatenate([near, rows], 1))
        others = jnp.where(core == 0, jnp.concatenate([far, far_near], 1), jnp.concatenate([far_near, far], 1))
        return jnp.where(z == 0, jnp.concatenate([mine, others], 1), jnp.concatenate([others, mine], 1))

    stored = whole(stored_hidden)
    weights = [slab(0).reshape(NZ * NC * local, HD)] + [
        along_x(slab(d), d).reshape(NZ * NC * local, HD) for d in range(1, NX)
    ]
    turn = whole(turn_hidden)

    s_own, s_terms, s_total = collect(stored, weights)
    t_own, t_terms, t_total = collect(turn, weights)

    positions = (block_start[:, None] + offsets[None, :]).reshape(-1)
    cosine, sine = angles(positions)
    pre = finish(s_own, s_terms, s_total, kv_bias)
    roped = rotate(pre, cosine, sine, is_key)
    keep = (offsets[None, :] < block_valid[:, None]).reshape(-1, 1)
    restored = jnp.where(keep, roped, 0.0).astype(jnp.bfloat16).reshape(blocks_here, BLK, HD)
    picks = (block_owner[:, None] == jnp.arange(groups)[None, :]).astype(jnp.bfloat16)
    outgoing = jnp.einsum(
        "bg,brd->grd", picks, restored, preferred_element_type=jnp.float32
    ).astype(jnp.bfloat16)
    arrived = lax.all_to_all(outgoing, "pool", split_axis=0, concat_axis=0, tiled=True)
    restored_cache = arrived.reshape(groups * BLK, HD)

    cosine, sine = angles(turn_position)
    pre = finish(t_own, t_terms, t_total, kv_bias)
    turn_kv = rotate(pre, cosine, sine, is_key).astype(jnp.bfloat16)
    return (restored_cache, turn_kv)


def solution(mesh):
    placed = (
        P("pool", "mp"),
        P("pool"),
        P("pool"),
        P("pool"),
        P("pool", "mp"),
        P("pool"),
        P(None, "mp"),
        P("mp"),
    )
    return jax.shard_map(
        shards,
        mesh=mesh,
        in_specs=placed,
        out_specs=(P("pool", "mp"), P("pool", "mp")),
        check_vma=False,
    )
```

```python
import jax
import jax.numpy as jnp
from jax import lax
from jax.experimental import pallas as pl
from jax.experimental.pallas import tpu as pltpu
from jax.sharding import PartitionSpec as P

D = 8192
HD = 128
BLK = 64
KVD = 1024
NZ = 2
NX = 4
NC = 2
SLAB = D // NX
LIFT = 16384.0
STEPS = 2048.0
TILE = 256
LN2 = 0.6931471805599453
LOW = 1e-36
HIGH = 1e37


def spot(z, x, c):
    return (z * NX + x) * NC + c


def pairs(move):
    return [
        (spot(z, x, c), spot(*move(z, x, c)))
        for z in range(NZ)
        for x in range(NX)
        for c in range(NC)
    ]


def to_z(v):
    return lax.ppermute(v, "mp", pairs(lambda z, x, c: (1 - z, x, c)))


def to_core(v):
    return lax.ppermute(v, "mp", pairs(lambda z, x, c: (z, x, 1 - c)))


def along_x(v, d):
    return lax.ppermute(v, "mp", pairs(lambda z, x, c: (z, (x + d) % NX, c)))


VMEM = pl.BlockSpec(memory_space=pltpu.VMEM)
SMEM = pl.BlockSpec(memory_space=pltpu.SMEM)
f32 = jnp.float32


def diagonal():
    shape = (HD, HD)
    return lax.broadcasted_iota(jnp.int32, shape, 0) == lax.broadcasted_iota(jnp.int32, shape, 1)


def anchor_kernel(x, out):
    out[...] = x[...]


def anchor(x):
    return pl.pallas_call(
        anchor_kernel,
        out_shape=jax.ShapeDtypeStruct(x.shape, x.dtype),
        in_specs=[VMEM],
        out_specs=VMEM,
        cost_estimate=pl.CostEstimate(flops=10**11, bytes_accessed=3 * 10**8, transcendentals=0),
    )(x)


def outer_kernel(home, r0, r1, r2, r3, w1, w3, f1, f3, code, norm):
    rows = norm.shape[0]
    mask = diagonal()

    def step(t, carry):
        at = pl.ds(pl.multiple_of(t * TILE, TILE), TILE)
        acc = jnp.zeros((TILE, 2 * HD), f32)
        sq = jnp.zeros((TILE, HD), f32)
        for j, r in enumerate((r0, r1, r2, r3)):
            piece = r[at, :]
            at_w = lax.bitwise_xor(home[0], j)
            acc += jnp.dot(
                piece, jnp.concatenate([w1[at_w], w3[at_w]], axis=1), preferred_element_type=f32
            )
            wide = piece.astype(f32)
            wide = wide * wide
            for k in range(wide.shape[1] // HD):
                sq += wide[:, k * HD : (k + 1) * HD]
        total = jnp.clip(jnp.sum(sq, axis=1, keepdims=True), LOW, HIGH)
        norm[at, :] = total
        down = LIFT * lax.rsqrt(total)
        f1[at, :] = acc[:, :HD] * down
        f3[at, :] = acc[:, HD:] * down
        return carry

    lax.fori_loop(0, rows // TILE, step, 0)
    lines = [
        jnp.sum(jnp.where(mask, norm[k * HD : (k + 1) * HD, :], 0.0), axis=0, keepdims=True)
        for k in range(rows // HD)
    ]
    u = jnp.log(jnp.concatenate(lines, axis=0)) * (1.0 / LN2)
    whole = jnp.floor(u)
    part = (u - whole) * STEPS
    middle = jnp.floor(part)
    told = jnp.concatenate([whole, middle, part - middle, jnp.zeros_like(u)], axis=0)
    code[...] = told
    f1[pl.ds(rows, 16), :] = told
    f3[pl.ds(rows, 16), :] = told


def inner_kernel(home, r0, r1, r2, r3, w0, w2, code, norm, own, f2):
    rows = norm.shape[0]

    def step(t, carry):
        at = pl.ds(pl.multiple_of(t * TILE, TILE), TILE)
        acc = jnp.zeros((TILE, 2 * HD), f32)
        for j, r in enumerate((r0, r1, r2, r3)):
            at_w = lax.bitwise_xor(home[0], j)
            acc += jnp.dot(
                r[at, :], jnp.concatenate([w0[at_w], w2[at_w]], axis=1), preferred_element_type=f32
            )
        own[at, :] = acc[:, :HD]
        f2[at, :] = acc[:, HD:] * (LIFT * lax.rsqrt(norm[at, :]))
        return carry

    lax.fori_loop(0, rows // TILE, step, 0)
    f2[pl.ds(rows, 16), :] = code[...]


def call(body, out, args, flops, scalars=0):
    return pl.pallas_call(
        body,
        out_shape=out,
        in_specs=[SMEM] * scalars + [VMEM] * (len(args) - scalars),
        out_specs=jax.tree.map(lambda _: VMEM, out),
        compiler_params=pltpu.CompilerParams(vmem_limit_bytes=24 * 2**20),
        cost_estimate=pl.CostEstimate(flops=flops, bytes_accessed=2**20, transcendentals=0),
    )(*args)


def outer(home, rows, w1, w3):
    count = rows[0].shape[0]
    sent = jax.ShapeDtypeStruct((count + 16, HD), f32)
    out = (
        sent,
        sent,
        jax.ShapeDtypeStruct((16, HD), f32),
        jax.ShapeDtypeStruct((count, 1), f32),
    )
    f1, f3, code, norm = call(outer_kernel, out, (home, *rows, w1, w3), 4 * count * HD * SLAB, 1)
    return f1.astype(jnp.float16), f3.astype(jnp.float16), code, norm


def inner(home, rows, w0, w2, code, norm):
    count = rows[0].shape[0]
    out = (
        jax.ShapeDtypeStruct((count, HD), f32),
        jax.ShapeDtypeStruct((count + 16, HD), f32),
    )
    own, f2 = call(inner_kernel, out, (home, *rows, w0, w2, code, norm), 4 * count * HD * SLAB, 1)
    return own, f2.astype(jnp.float16)


def finished(k, mask, own, code, got, bias, cosine, sine):
    at = slice(k * HD, (k + 1) * HD)
    lines = own.shape[0] // HD

    def norm_line(ref, first):
        u = ref[first + k : first + k + 1, :] + (
            ref[first + lines + k : first + lines + k + 1, :]
            + ref[first + 2 * lines + k : first + 2 * lines + k + 1, :]
        ) * (1.0 / STEPS)
        return jnp.exp(u * LN2)

    def column(line):
        return jnp.sum(jnp.where(mask, line, 0.0), axis=1, keepdims=True)

    norms = [norm_line(g, own.shape[0]) for g in got]
    total = norm_line(code, 0) + norms[0] + norms[1] + norms[2]
    scale = lax.rsqrt(total / D + 1e-06)
    value = own[at, :] * column(scale) + bias[...]
    for g, n in zip(got, norms):
        value += g[at, :] * column(jnp.sqrt(n) * scale * (1.0 / LIFT))
    return value * cosine[at, :] + pltpu.roll(value, HD // 2, 1) * sine[at, :]


def turn_kernel(own, code, g1, g2, g3, bias, cosine, sine, out):
    mask = diagonal()
    for k in range(own.shape[0] // HD):
        value = finished(k, mask, own, code, (g1, g2, g3), bias, cosine, sine)
        out[k * HD : (k + 1) * HD, :] = value.astype(out.dtype)


def stored_kernel(owner, valid, own, code, g1, g2, g3, bias, cosine, sine, out):
    mask = diagonal()
    row = lax.broadcasted_iota(jnp.int32, (BLK, HD), 0)
    out[...] = jnp.zeros(out.shape, out.dtype)
    for k in range(own.shape[0] // HD):
        value = finished(k, mask, own, code, (g1, g2, g3), bias, cosine, sine)
        for h in range(HD // BLK):
            b = k * (HD // BLK) + h
            kept = jnp.where(row < valid[b], value[h * BLK : (h + 1) * BLK], 0.0)
            out[owner[b]] = kept.astype(out.dtype)


def tables(positions, is_key):
    half = HD // 2
    freq = jnp.exp(
        -jnp.log(jnp.float32(1000000.0)) * (jnp.arange(half).astype(jnp.float32) * 2.0 / HD)
    )
    angle = positions.astype(jnp.float32)[:, None] * jnp.concatenate([freq, freq])[None, :]
    sign = jnp.where(jnp.arange(HD) < half, -1.0, 1.0)
    return (
        jnp.where(is_key, jnp.cos(angle), 1.0),
        jnp.where(is_key, jnp.sin(angle) * sign[None, :], 0.0),
    )


def shards(
    stored_hidden,
    block_owner,
    block_valid,
    block_start,
    turn_hidden,
    turn_position,
    kv_weight,
    kv_bias,
):
    groups = lax.axis_size("pool")
    me = lax.axis_index("mp")
    x = (me // NC) % NX
    z = me // (NC * NX)
    core = me % NC
    is_key = me * HD < KVD
    count, local = stored_hidden.shape
    bias = kv_bias[None, :]

    chunks = kv_weight.reshape(NZ, NX, NC, local, HD)

    home = (z * NC + core).astype(jnp.int32)[None]

    def slab(d):
        part = lax.dynamic_index_in_dim(chunks, (x + d) % NX, axis=1, keepdims=False)
        return part.reshape(NZ * NC, local, HD)

    held = anchor(bias)
    s_far = to_z(stored_hidden)
    w1 = along_x(slab(1), 1)
    w3 = along_x(slab(3), 3)
    w2 = along_x(slab(2), 2)
    near_in, bias = lax.optimization_barrier((stored_hidden, held))
    s_near = to_core(near_in)
    far_in, turn_in, _ = lax.optimization_barrier((s_far, turn_hidden, held))
    s_far_near = to_core(far_in)
    t_far = to_z(turn_in)
    t_near = to_core(turn_in)
    t_far_near = to_core(t_far)
    w0 = slab(0)

    s_rows = (stored_hidden, s_near, s_far, s_far_near)
    s1, s3, s_code, s_norm = outer(home, s_rows, w1, w3)
    s_g1, s_g3 = along_x(s1, NX - 1), along_x(s3, NX - 3)
    s_own, s2 = inner(home, s_rows, w0, w2, s_code, s_norm)
    s_g2 = along_x(s2, NX - 2)

    t_rows = (turn_hidden, t_near, t_far, t_far_near)
    t1, t3, t_code, t_norm = outer(home, t_rows, w1, w3)
    t_own, t2 = inner(home, t_rows, w0, w2, t_code, t_norm)
    s_own, t1, t2, t3 = lax.optimization_barrier((s_own, t1, t2, t3))

    positions = (block_start[:, None] + jnp.arange(BLK)[None, :]).reshape(-1)
    args = [v.astype(f32) for v in (s_g1, s_g2, s_g3)]
    outgoing = call(
        stored_kernel,
        jax.ShapeDtypeStruct((groups, BLK, HD), jnp.bfloat16),
        (block_owner, block_valid, s_own, s_code, *args, bias, *tables(positions, is_key)),
        2**20,
        2,
    )
    arrived = lax.all_to_all(outgoing, "pool", split_axis=0, concat_axis=0, tiled=True)
    restored_cache = arrived.reshape(groups * BLK, HD)

    t_got = along_x(t1, NX - 1), along_x(t2, NX - 2), along_x(t3, NX - 3)
    args = [v.astype(f32) for v in t_got]
    turn_kv = call(
        turn_kernel,
        jax.ShapeDtypeStruct((count, HD), jnp.bfloat16),
        (t_own, t_code, *args, bias, *tables(turn_position, is_key)),
        2**20,
    )
    return (restored_cache, turn_kv)


def solution(mesh):
    placed = (
        P("pool", "mp"),
        P("pool"),
        P("pool"),
        P("pool"),
        P("pool", "mp"),
        P("pool"),
        P(None, "mp"),
        P("mp"),
    )
    return jax.shard_map(
        shards,
        mesh=mesh,
        in_specs=placed,
        out_specs=(P("pool", "mp"), P("pool", "mp")),
        check_vma=False,
    )
```

```python
import functools

import jax
import jax.numpy as jnp
from jax import lax
from jax.experimental import pallas as pl
from jax.experimental.pallas import tpu as pltpu
from jax.sharding import PartitionSpec as P

D = 8192
HD = 128
BLK = 64
KVD = 1024
NZ = 2
NX = 4
NC = 2
NY = 4
LIFT = 16384.0
STEPS = 2048.0
LN2 = 0.6931471805599453
LOW = 1e-36
HIGH = 1e37


def spot(z, x, c):
    return (z * NX + x) * NC + c


def pairs(move):
    return [
        (spot(z, x, c), spot(*move(z, x, c)))
        for z in range(NZ)
        for x in range(NX)
        for c in range(NC)
    ]


def across(v, e):
    return lax.ppermute(v, "mp", pairs(lambda z, x, c: (z ^ (e // NC), x, c ^ (e % NC))))


def outward(v, groups):
    ring = groups // NY
    moves = []
    for h in range(ring):
        for y in range(NY):
            for z, x, c in ((z, x, c) for z in range(NZ) for x in range(NX) for c in range(NC)):
                g = (h + 2 * z - 1) % ring * NY + y
                src = (h * NY + y) * NZ * NX * NC + spot(z, x, c)
                moves.append((src, g * NZ * NX * NC + spot(1 - z, x, 1 - c)))
    return lax.ppermute(v, ("pool", "mp"), moves)


def along_x(v, d):
    return lax.ppermute(v, "mp", pairs(lambda z, x, c: (z, (x + d) % NX, c)))


VMEM = pl.BlockSpec(memory_space=pltpu.VMEM)
SMEM = pl.BlockSpec(memory_space=pltpu.SMEM)
HBM = pl.BlockSpec(memory_space=pltpu.HBM)
f32 = jnp.float32


def diagonal():
    shape = (HD, HD)
    return lax.broadcasted_iota(jnp.int32, shape, 0) == lax.broadcasted_iota(jnp.int32, shape, 1)


def place():
    me = lax.axis_index("mp")
    return me // (NC * NX), lax.rem(me // NC, NX), lax.rem(me, NC)


def slice_kernel(w, w1, w2, w3, sems):
    z, _, c = place()
    copies = []
    for e, out in ((2, w2), (3, w3), (1, w1)):
        for k in range(NX):
            src = w.at[lax.bitwise_xor(z, e // NC), k, lax.bitwise_xor(c, e % NC)]
            copies.append(pltpu.make_async_copy(src, out.at[k], sems.at[len(copies)]))
    for copy in copies:
        copy.start()
    for copy in copies:
        copy.wait()


def slices(w):
    part = jax.ShapeDtypeStruct((NX,) + w.shape[3:], w.dtype)
    return pl.pallas_call(
        slice_kernel,
        out_shape=(part,) * 3,
        in_specs=[pl.BlockSpec(memory_space=pl.ANY)],
        out_specs=(VMEM,) * 3,
        scratch_shapes=[pltpu.SemaphoreType.DMA((3 * NX,))],
        cost_estimate=pl.CostEstimate(flops=0, bytes_accessed=2**21, transcendentals=0),
    )(w)


def anchor_kernel(x, after, out):
    out[...] = x[...]


def anchor(x, after):
    return pl.pallas_call(
        anchor_kernel,
        out_shape=jax.ShapeDtypeStruct(x.shape, x.dtype),
        in_specs=[VMEM, pl.BlockSpec(memory_space=pl.ANY)],
        out_specs=VMEM,
        compiler_params=pltpu.CompilerParams(vmem_limit_bytes=2**20),
        cost_estimate=pl.CostEstimate(flops=10**11, bytes_accessed=3 * 10**8, transcendentals=0),
    )(x, after)


def load(w, weights, wv, ws, order):
    z, x, c = place()
    waits = {}
    for j in order:
        k = lax.rem(x - j + NX, NX)
        waits[j] = []
        for e, src in enumerate((w.at[z, k, c], *(v.at[k] for v in weights))):
            copy = pltpu.make_async_copy(src, wv.at[j, e], ws.at[j * 4 + e])
            copy.start()
            waits[j].append(copy)
    return waits


def product(piece, wv, j):
    both = jnp.concatenate([wv[j, e] for e in range(4)], axis=1)
    return jnp.dot(piece, both, preferred_element_type=f32)


def squared(piece):
    wide = piece.astype(f32)
    wide = wide * wide
    return sum(wide[:, g * HD : (g + 1) * HD] for g in range(wide.shape[1] // HD))


def first_kernel(r0, r1, r3, w, w1, w2, w3, acc, sq, rv, wv, rs, ws):
    rows = {0: r0, 1: r1, 3: r3}
    copies = {}
    for j, r in rows.items():
        copies[j] = pltpu.make_async_copy(r, rv.at[j], rs.at[j])
        copies[j].start()
    waits = load(w, (w1, w2, w3), wv, ws, rows)
    for j in rows:
        copies[j].wait()
        for copy in waits[j]:
            copy.wait()
        if j == 0:
            acc[...] = product(rv[j], wv, j)
            sq[...] = squared(rv[j])
        else:
            acc[...] += product(rv[j], wv, j)
            sq[...] += squared(rv[j])


def last_kernel(count, *refs):
    pieces, refs = refs[:count], refs[count:]
    w, w1, w2, w3, acc, sq, own, f1, f2, f3, code, rv, wv, rs, ws = refs
    size = own.shape[0] // count
    copies = []
    for n, r in enumerate(pieces):
        at = pl.ds(n * size, size)
        copies.append(pltpu.make_async_copy(r, rv.at[2, at], rs.at[n]))
        copies[n].start()
    waits = load(w, (w1, w2, w3), wv, ws, (2,))
    for copy in copies + waits[2]:
        copy.wait()
    total = acc[...] + product(rv[2], wv, 2)
    pack(total, sq[...] + squared(rv[2]), own, f1, f2, f3, code)


def whole_kernel(r0, r1, r2, r3, w, w1, w2, w3, own, f1, f2, f3, code, rv, wv, rs, ws):
    rows = (r0, r1, r2, r3)
    copies = []
    for j, r in enumerate(rows):
        copies.append(pltpu.make_async_copy(r, rv.at[j], rs.at[j]))
        copies[j].start()
    waits = load(w, (w1, w2, w3), wv, ws, range(NX))
    total = sq = 0.0
    for j in range(NX):
        copies[j].wait()
        for copy in waits[j]:
            copy.wait()
        total += product(rv[j], wv, j)
        sq += squared(rv[j])
    pack(total, sq, own, f1, f2, f3, code)


def pack(total, sq, own, f1, f2, f3, code):
    rows = own.shape[0]
    mask = diagonal()
    norm = jnp.clip(jnp.sum(sq, axis=1, keepdims=True), LOW, HIGH)
    down = LIFT * lax.rsqrt(norm)
    own[...] = total[:, :HD]
    for e, f in enumerate((f1, f2, f3)):
        f[pl.ds(0, rows), :] = total[:, (e + 1) * HD : (e + 2) * HD] * down
    lines = []
    for g in range(rows // HD):
        part = jnp.where(mask, norm[g * HD : (g + 1) * HD, :], 0.0)
        lines.append(jnp.sum(part, axis=0, keepdims=True))
    u = jnp.log(jnp.concatenate(lines, axis=0)) * (1.0 / LN2)
    whole = jnp.floor(u)
    part = (u - whole) * STEPS
    middle = jnp.floor(part)
    told = jnp.concatenate([whole, middle, part - middle, jnp.zeros_like(u)], axis=0)
    code[...] = told
    for f in (f1, f2, f3):
        f[pl.ds(rows, 16), :] = told


def scratch(rows, w):
    return [
        pltpu.VMEM((NX,) + rows, w.dtype),
        pltpu.VMEM((NX, 4) + w.shape[3:], w.dtype),
        pltpu.SemaphoreType.DMA((NX,)),
        pltpu.SemaphoreType.DMA((NX * 4,)),
    ]


def multiply(body, rows, w, weights, held, out, grant, cost):
    count, local = rows[0].shape[0], rows[0].shape[1]
    return pl.pallas_call(
        body,
        out_shape=out,
        in_specs=[HBM] * (len(rows) + 4) + [VMEM] * len(held),
        out_specs=(VMEM,) * len(out),
        scratch_shapes=scratch((out[0].shape[0], local), w),
        compiler_params=pltpu.CompilerParams(vmem_limit_bytes=grant * 2**20),
        cost_estimate=pl.CostEstimate(flops=cost * 2**30, bytes_accessed=2**22, transcendentals=0),
    )(*rows, w, *weights, *held)


def outputs(count):
    sent = jax.ShapeDtypeStruct((count + 16, HD), f32)
    return (
        jax.ShapeDtypeStruct((count, HD), f32),
        sent,
        sent,
        sent,
        jax.ShapeDtypeStruct((16, HD), f32),
    )


def half_width(parts):
    own, f1, f2, f3, code = parts
    return own, code, [f.astype(jnp.float16) for f in (f1, f2, f3)]


def call(body, out, args, flops, scalars=0):
    return pl.pallas_call(
        body,
        out_shape=out,
        in_specs=[SMEM] * scalars + [VMEM] * (len(args) - scalars),
        out_specs=jax.tree.map(lambda _: VMEM, out),
        compiler_params=pltpu.CompilerParams(vmem_limit_bytes=12 * 2**20),
        cost_estimate=pl.CostEstimate(flops=flops, bytes_accessed=2**20, transcendentals=0),
    )(*args)


def columns(own, code, got):
    lines = own.shape[0] // HD

    def norms_of(ref, first):
        u = ref[first : first + lines, :] + (
            ref[first + lines : first + 2 * lines, :]
            + ref[first + 2 * lines : first + 3 * lines, :]
        ) * (1.0 / STEPS)
        return jnp.exp(u * LN2)

    norms = [norms_of(g, own.shape[0]) for g in got]
    total = norms_of(code, 0) + norms[0] + norms[1] + norms[2]
    scale = lax.rsqrt(total / D + 1e-06)
    ups = [jnp.sqrt(n) * scale * (1.0 / LIFT) for n in norms]
    rest = jnp.zeros((HD - 4 * lines, HD), f32)
    return jnp.concatenate([scale, *ups, rest], axis=0).T


def finished(k, cols, own, got, bias, cosine, sine):
    at = slice(k * HD, (k + 1) * HD)
    lines = own.shape[0] // HD
    value = own[at, :] * cols[:, k : k + 1] + bias[...]
    for d, g in enumerate(got):
        j = (d + 1) * lines + k
        value += g[at, :] * cols[:, j : j + 1]
    return value * cosine[at, :] + pltpu.roll(value, HD // 2, 1) * sine[at, :]


def turn_kernel(arrived, own, code, g1, g2, g3, bias, cosine, sine, out, cache, held, sems):
    take = pltpu.make_async_copy(arrived, held, sems.at[0])
    take.start()
    cols = columns(own, code, (g1, g2, g3))
    give = pltpu.make_async_copy(held, cache, sems.at[1])
    for k in range(own.shape[0] // HD):
        value = finished(k, cols, own, (g1, g2, g3), bias, cosine, sine)
        out[k * HD : (k + 1) * HD, :] = value.astype(out.dtype)
        if k == 0:
            take.wait()
            give.start()
    give.wait()


def stored_kernel(owner, valid, own, code, g1, g2, g3, bias, cosine, sine, out):
    row = lax.broadcasted_iota(jnp.int32, (BLK, HD), 0)
    out[...] = jnp.zeros(out.shape, out.dtype)
    cols = columns(own, code, (g1, g2, g3))
    for k in range(own.shape[0] // HD):
        value = finished(k, cols, own, (g1, g2, g3), bias, cosine, sine)
        for h in range(HD // BLK):
            b = k * (HD // BLK) + h
            kept = jnp.where(row < valid[b], value[h * BLK : (h + 1) * BLK], 0.0)
            out[owner[b]] = kept.astype(out.dtype)


def tables(positions, is_key):
    half = HD // 2
    freq = jnp.exp(
        -jnp.log(jnp.float32(1000000.0)) * (jnp.arange(half).astype(jnp.float32) * 2.0 / HD)
    )
    angle = positions.astype(jnp.float32)[:, None] * jnp.concatenate([freq, freq])[None, :]
    sign = jnp.where(jnp.arange(HD) < half, -1.0, 1.0)
    return (
        jnp.where(is_key, jnp.cos(angle), 1.0),
        jnp.where(is_key, jnp.sin(angle) * sign[None, :], 0.0),
    )


def shards(
    stored_hidden,
    block_owner,
    block_valid,
    block_start,
    turn_hidden,
    turn_position,
    kv_weight,
    kv_bias,
):
    groups = lax.axis_size("pool")
    me = lax.axis_index("mp")
    is_key = me * HD < KVD
    count, local = stored_hidden.shape
    bias = kv_bias[None, :]

    chunks = kv_weight.reshape(NZ, NX, NC, local, HD)

    positions = (block_start[:, None] + jnp.arange(BLK)[None, :]).reshape(-1)
    s_tables = tables(positions, is_key)
    t_tables = tables(turn_position, is_key)

    s1 = along_x(stored_hidden, 1)
    s3 = along_x(stored_hidden, 3)
    parts = slices(chunks)
    held = anchor(bias, parts[0])
    w1, w2, w3 = parts
    w2 = across(w2, 2)
    w3 = outward(w3, groups)
    s1, s3, w1 = lax.optimization_barrier((s1, s3, w1))
    w1 = across(w1, 1)
    weights = [w1, w2, w3]
    half = count // 2
    s1, s3, s_tables, t_tables = lax.optimization_barrier((s1, s3, s_tables, t_tables))
    s2a = along_x(s1[:half], 1)
    s2b = along_x(s3[half:], 3)
    row, s1, s3, bias = lax.optimization_barrier((turn_hidden, s1, s3, held))
    t1 = along_x(row, 1)
    t3 = along_x(row, 3)
    partly = (
        jax.ShapeDtypeStruct((count, 4 * HD), f32),
        jax.ShapeDtypeStruct((count, HD), f32),
    )
    acc, sq = multiply(first_kernel, (stored_hidden, s1, s3), chunks, weights, (), partly, 16,1)
    last = functools.partial(last_kernel, 2)
    parts = multiply(last, (s2a, s2b), chunks, weights, (acc, sq), outputs(count), 16,1)
    s_own, s_code, s_sent = half_width(parts)
    s_g1, s_g2, s_g3 = [across(v, e) for e, v in zip((1, 2, 3), s_sent)]
    row, s_code = lax.optimization_barrier((turn_hidden, s_code))
    t2 = along_x(row, 2)
    t_rows = [turn_hidden, t1, t2, t3]

    args = [v.astype(f32) for v in (s_g1, s_g2, s_g3)]
    outgoing = call(
        stored_kernel,
        jax.ShapeDtypeStruct((groups, BLK, HD), jnp.bfloat16),
        (block_owner, block_valid, s_own, s_code, *args, bias, *s_tables),
        2**20,
        2,
    )
    arrived = lax.all_to_all(outgoing, "pool", split_axis=0, concat_axis=0, tiled=True)

    t_rows[0], outgoing = lax.optimization_barrier((t_rows[0], outgoing))
    parts = multiply(whole_kernel, t_rows, chunks, weights, (), outputs(count), 16,2)
    t_own, t_code, t_sent = half_width(parts)
    t1, t2, t3 = t_sent
    t_got = across(t1, 1), across(t2, 2), across(t3, 3)
    args = [v.astype(f32) for v in t_got]
    args = (arrived, t_own, t_code, *args, bias, *t_tables)
    cache = jax.ShapeDtypeStruct(arrived.shape, arrived.dtype)
    turn_kv, restored = pl.pallas_call(
        turn_kernel,
        out_shape=(jax.ShapeDtypeStruct((count, HD), jnp.bfloat16), cache),
        in_specs=[pl.BlockSpec(memory_space=pl.ANY)] + [VMEM] * (len(args) - 1),
        out_specs=(VMEM, pl.BlockSpec(memory_space=pl.ANY)),
        scratch_shapes=[pltpu.VMEM(arrived.shape, arrived.dtype), pltpu.SemaphoreType.DMA((2,))],
        compiler_params=pltpu.CompilerParams(vmem_limit_bytes=12 * 2**20),
        cost_estimate=pl.CostEstimate(flops=2**20, bytes_accessed=2**20, transcendentals=0),
    )(*args)
    return (restored.reshape(groups * BLK, HD), turn_kv)


def solution(mesh):
    placed = (
        P("pool", "mp"),
        P("pool"),
        P("pool"),
        P("pool"),
        P("pool", "mp"),
        P("pool"),
        P(None, "mp"),
        P("mp"),
    )
    return jax.shard_map(
        shards,
        mesh=mesh,
        in_specs=placed,
        out_specs=(P("pool", "mp"), P("pool", "mp")),
        check_vma=False,
    )
```

```python
import functools

import jax
import jax.numpy as jnp
from jax import lax
from jax.experimental import pallas as pl
from jax.experimental.pallas import tpu as pltpu
from jax.sharding import PartitionSpec as P

D = 8192
HD = 128
BLK = 64
KVD = 1024
NZ = 2
NX = 4
NC = 2
NY = 4
LIFT = 16384.0
STEPS = 2048.0
LN2 = 0.6931471805599453
LOW = 1e-36
HIGH = 1e37


def spot(z, x, c):
    return (z * NX + x) * NC + c


def pairs(move):
    return [
        (spot(z, x, c), spot(*move(z, x, c)))
        for z in range(NZ)
        for x in range(NX)
        for c in range(NC)
    ]


def across(v, e):
    return lax.ppermute(v, "mp", pairs(lambda z, x, c: (z ^ (e // NC), x, c ^ (e % NC))))


def outward(v, groups):
    ring = groups // NY
    moves = []
    for h in range(ring):
        for y in range(NY):
            for z, x, c in ((z, x, c) for z in range(NZ) for x in range(NX) for c in range(NC)):
                g = (h + 2 * z - 1) % ring * NY + y
                src = (h * NY + y) * NZ * NX * NC + spot(z, x, c)
                moves.append((src, g * NZ * NX * NC + spot(1 - z, x, 1 - c)))
    return lax.ppermute(v, ("pool", "mp"), moves)


def along_x(v, d):
    return lax.ppermute(v, "mp", pairs(lambda z, x, c: (z, (x + d) % NX, c)))


VMEM = pl.BlockSpec(memory_space=pltpu.VMEM)
SMEM = pl.BlockSpec(memory_space=pltpu.SMEM)
ANY = pl.BlockSpec(memory_space=pl.ANY)
f32 = jnp.float32


def diagonal():
    shape = (HD, HD)
    return lax.broadcasted_iota(jnp.int32, shape, 0) == lax.broadcasted_iota(jnp.int32, shape, 1)


def place():
    me = lax.axis_index("mp")
    return me // (NC * NX), lax.rem(me // NC, NX), lax.rem(me, NC)


def slice_kernel(w, w1, w2, w3, sems):
    z, _, c = place()
    copies = []
    for e, out in ((2, w2), (3, w3), (1, w1)):
        for k in range(NX):
            src = w.at[lax.bitwise_xor(z, e // NC), k, lax.bitwise_xor(c, e % NC)]
            copies.append(pltpu.make_async_copy(src, out.at[k], sems.at[len(copies)]))
    for copy in copies:
        copy.start()
    for copy in copies:
        copy.wait()


def slices(w):
    part = jax.ShapeDtypeStruct((NX,) + w.shape[3:], w.dtype)
    return pl.pallas_call(
        slice_kernel,
        out_shape=(part,) * 3,
        in_specs=[pl.BlockSpec(memory_space=pl.ANY)],
        out_specs=(VMEM,) * 3,
        scratch_shapes=[pltpu.SemaphoreType.DMA((3 * NX,))],
        cost_estimate=pl.CostEstimate(flops=0, bytes_accessed=2**21, transcendentals=0),
    )(w)


def anchor_kernel(x, after, out):
    out[...] = x[...]


def anchor(x, after):
    return pl.pallas_call(
        anchor_kernel,
        out_shape=jax.ShapeDtypeStruct(x.shape, x.dtype),
        in_specs=[VMEM, pl.BlockSpec(memory_space=pl.ANY)],
        out_specs=VMEM,
        compiler_params=pltpu.CompilerParams(vmem_limit_bytes=2**20),
        cost_estimate=pl.CostEstimate(flops=10**11, bytes_accessed=3 * 10**8, transcendentals=0),
    )(x, after)


def product(piece, j, weights, w0):
    _, x, _ = place()
    k = lax.rem(x - j + NX, NX)
    both = jnp.concatenate([w0[j]] + [w[k] for w in weights], axis=1)
    return jnp.dot(piece, both, preferred_element_type=f32)


def squared(piece):
    wide = piece.astype(f32)
    wide = wide * wide
    return sum(wide[:, g * HD : (g + 1) * HD] for g in range(wide.shape[1] // HD))


def fetch(w, w0, sems, order):
    z, x, c = place()
    copies = {}
    for j in order:
        src = w.at[z, lax.rem(x - j + NX, NX), c]
        copies[j] = pltpu.make_async_copy(src, w0.at[j], sems.at[j])
        copies[j].start()
    return copies


def first_kernel(w, r0, r1, r3, w1, w2, w3, acc, sq, w0, sems):
    rows = {0: r0, 1: r1, 3: r3}
    copies = fetch(w, w0, sems, rows)
    for j, r in rows.items():
        copies[j].wait()
        if j == 0:
            acc[...] = product(r[...], j, (w1, w2, w3), w0)
            sq[...] = squared(r[...])
        else:
            acc[...] += product(r[...], j, (w1, w2, w3), w0)
            sq[...] += squared(r[...])


def last_kernel(count, w, *refs):
    pieces, refs = refs[:count], refs[count:]
    w1, w2, w3, acc, sq, own, f1, f2, f3, code, w0, sems = refs
    fetch(w, w0, sems, (2,))[2].wait()
    piece = jnp.concatenate([r[...] for r in pieces], axis=0)
    total = acc[...] + product(piece, 2, (w1, w2, w3), w0)
    pack(total, sq[...] + squared(piece), own, f1, f2, f3, code)


def whole_kernel(w, r0, r1, r2, r3, w1, w2, w3, own, f1, f2, f3, code, w0, sems, rv, rs):
    order = (0, 1, 3, 2)
    moves = {}
    for j, r in enumerate((r0, r1, r2, r3)):
        moves[j] = pltpu.make_async_copy(r, rv.at[j], rs.at[j])
    moves[0].start()
    copies = fetch(w, w0, sems, order)
    for j in order[1:]:
        moves[j].start()
    total = sq = 0.0
    for j in order:
        copies[j].wait()
        moves[j].wait()
        total += product(rv[j], j, (w1, w2, w3), w0)
        sq += squared(rv[j])
    pack(total, sq, own, f1, f2, f3, code)


def pack(total, sq, own, f1, f2, f3, code):
    rows = own.shape[0]
    mask = diagonal()
    norm = jnp.clip(jnp.sum(sq, axis=1, keepdims=True), LOW, HIGH)
    down = LIFT * lax.rsqrt(norm)
    own[...] = total[:, :HD]
    for e, f in enumerate((f1, f2, f3)):
        f[pl.ds(0, rows), :] = total[:, (e + 1) * HD : (e + 2) * HD] * down
    lines = []
    for g in range(rows // HD):
        part = jnp.where(mask, norm[g * HD : (g + 1) * HD, :], 0.0)
        lines.append(jnp.sum(part, axis=0, keepdims=True))
    u = jnp.log(jnp.concatenate(lines, axis=0)) * (1.0 / LN2)
    whole = jnp.floor(u)
    part = (u - whole) * STEPS
    middle = jnp.floor(part)
    told = jnp.concatenate([whole, middle, part - middle, jnp.zeros_like(u)], axis=0)
    code[...] = told
    for f in (f1, f2, f3):
        f[pl.ds(rows, 16), :] = told


def multiply(body, rows, w, weights, held, out, grant, cost):
    stay = body is not whole_kernel
    moved = [pltpu.VMEM((NX,) + rows[0].shape, w.dtype), pltpu.SemaphoreType.DMA((NX,))]
    return pl.pallas_call(
        body,
        out_shape=out,
        in_specs=[ANY] + [VMEM if stay else ANY] * len(rows) + [VMEM] * (3 + len(held)),
        out_specs=(VMEM,) * len(out),
        scratch_shapes=[
            pltpu.VMEM((NX,) + w.shape[3:], w.dtype),
            pltpu.SemaphoreType.DMA((NX,)),
        ]
        + ([] if stay else moved),
        compiler_params=pltpu.CompilerParams(vmem_limit_bytes=grant * 2**20),
        cost_estimate=pl.CostEstimate(flops=cost * 2**30, bytes_accessed=2**22, transcendentals=0),
    )(w, *rows, *weights, *held)


def outputs(count):
    sent = jax.ShapeDtypeStruct((count + 16, HD), f32)
    return (
        jax.ShapeDtypeStruct((count, HD), f32),
        sent,
        sent,
        sent,
        jax.ShapeDtypeStruct((16, HD), f32),
    )


def half_width(parts):
    own, f1, f2, f3, code = parts
    return own, code, [f.astype(jnp.float16) for f in (f1, f2, f3)]


def call(body, out, args, flops, scalars=0):
    return pl.pallas_call(
        body,
        out_shape=out,
        in_specs=[SMEM] * scalars + [VMEM] * (len(args) - scalars),
        out_specs=jax.tree.map(lambda _: VMEM, out),
        compiler_params=pltpu.CompilerParams(vmem_limit_bytes=12 * 2**20),
        cost_estimate=pl.CostEstimate(flops=flops, bytes_accessed=2**20, transcendentals=0),
    )(*args)


def columns(own, code, got):
    lines = own.shape[0] // HD

    def norms_of(ref, first):
        u = ref[first : first + lines, :] + (
            ref[first + lines : first + 2 * lines, :]
            + ref[first + 2 * lines : first + 3 * lines, :]
        ) * (1.0 / STEPS)
        return jnp.exp(u * LN2)

    norms = [norms_of(g, own.shape[0]) for g in got]
    total = norms_of(code, 0) + norms[0] + norms[1] + norms[2]
    scale = lax.rsqrt(total / D + 1e-06)
    ups = [jnp.sqrt(n) * scale * (1.0 / LIFT) for n in norms]
    rest = jnp.zeros((HD - 4 * lines, HD), f32)
    return jnp.concatenate([scale, *ups, rest], axis=0).T


def finished(k, cols, own, got, bias, turns):
    at = slice(k * HD, (k + 1) * HD)
    lines = own.shape[0] // HD
    value = own[at, :] * cols[:, k : k + 1] + bias[...]
    for d, g in enumerate(got):
        j = (d + 1) * lines + k
        value += g[at, :] * cols[:, j : j + 1]
    turn = turns[at, :]
    swapped = pltpu.roll(turn, HD // 2, 1)
    first = lax.broadcasted_iota(jnp.int32, turn.shape, 1) < HD // 2
    cosine = jnp.where(first, turn, swapped)
    sine = jnp.where(first, -swapped, turn)
    return value * cosine + pltpu.roll(value, HD // 2, 1) * sine


def emit_kernel(arrived, cache):
    cache[...] = arrived[...]


def turn_kernel(own, code, g1, g2, g3, bias, turns, out):
    cols = columns(own, code, (g1, g2, g3))
    for k in range(own.shape[0] // HD):
        value = finished(k, cols, own, (g1, g2, g3), bias, turns)
        out[k * HD : (k + 1) * HD, :] = value.astype(out.dtype)


def stored_kernel(owner, valid, own, code, g1, g2, g3, bias, turns, out):
    row = lax.broadcasted_iota(jnp.int32, (BLK, HD), 0)
    out[...] = jnp.zeros(out.shape, out.dtype)
    cols = columns(own, code, (g1, g2, g3))
    for k in range(own.shape[0] // HD):
        value = finished(k, cols, own, (g1, g2, g3), bias, turns)
        for h in range(HD // BLK):
            b = k * (HD // BLK) + h
            kept = jnp.where(row < valid[b], value[h * BLK : (h + 1) * BLK], 0.0)
            out[owner[b]] = kept.astype(out.dtype)


def tables(positions, is_key):
    half = HD // 2
    freq = jnp.exp(
        -jnp.log(jnp.float32(1000000.0)) * (jnp.arange(half).astype(jnp.float32) * 2.0 / HD)
    )
    angle = positions.astype(jnp.float32)[:, None] * jnp.concatenate([freq, freq])[None, :]
    first = (jnp.arange(HD) < half)[None, :]
    plain = jnp.where(first, 1.0, 0.0)
    return jnp.where(is_key, jnp.where(first, jnp.cos(angle), jnp.sin(angle)), plain)


def shards(
    stored_hidden,
    block_owner,
    block_valid,
    block_start,
    turn_hidden,
    turn_position,
    kv_weight,
    kv_bias,
):
    groups = lax.axis_size("pool")
    me = lax.axis_index("mp")
    is_key = me * HD < KVD
    count, local = stored_hidden.shape
    bias = kv_bias[None, :]

    chunks = kv_weight.reshape(NZ, NX, NC, local, HD)

    positions = (block_start[:, None] + jnp.arange(BLK)[None, :]).reshape(-1)
    s_tables = tables(positions, is_key)
    t_tables = tables(turn_position, is_key)

    s1 = along_x(stored_hidden, 1)
    s3 = along_x(stored_hidden, 3)
    parts = slices(chunks)
    held = anchor(bias, parts[0])
    w1, w2, w3 = parts
    w2 = across(w2, 2)
    w3 = outward(w3, groups)
    w1, _ = lax.optimization_barrier((w1, s3))
    w1 = across(w1, 1)
    weights = [w1, w2, w3]
    half = count // 2
    s1, s_tables, t_tables = lax.optimization_barrier((s1, s_tables, t_tables))
    s2a = along_x(s1[:half], 1)
    s2b = along_x(s3[half:], 3)
    row, s1, s3, bias = lax.optimization_barrier((turn_hidden, s1, s3, held))
    t1 = along_x(row, 1)
    t3 = along_x(row, 3)
    partly = (
        jax.ShapeDtypeStruct((count, 4 * HD), f32),
        jax.ShapeDtypeStruct((count, HD), f32),
    )
    acc, sq = multiply(first_kernel, (stored_hidden, s1, s3), chunks, weights, (), partly, 16,1)
    row, acc = lax.optimization_barrier((turn_hidden, acc))
    t2 = along_x(row, 2)
    last = functools.partial(last_kernel, 2)
    parts = multiply(last, (s2a, s2b), chunks, weights, (acc, sq), outputs(count), 16,1)
    s_own, s_code, s_sent = half_width(parts)
    s_g1, s_g2, s_g3 = [across(v, e) for e, v in zip((1, 2, 3), s_sent)]
    t_rows = [turn_hidden, t1, t2, t3]

    args = [v.astype(f32) for v in (s_g1, s_g2, s_g3)]
    outgoing = call(
        stored_kernel,
        jax.ShapeDtypeStruct((groups, BLK, HD), jnp.bfloat16),
        (block_owner, block_valid, s_own, s_code, *args, bias, s_tables),
        2**20,
        2,
    )
    arrived = lax.all_to_all(outgoing, "pool", split_axis=0, concat_axis=0, tiled=True)

    t_rows[0], outgoing = lax.optimization_barrier((t_rows[0], outgoing))
    parts = multiply(whole_kernel, t_rows, chunks, weights, (), outputs(count), 16,2)
    t_own, t_code, t_sent = half_width(parts)
    t1, t2, t3 = t_sent
    t_got = across(t1, 1), across(t2, 2), across(t3, 3)
    args = [v.astype(f32) for v in t_got]
    shape = jax.ShapeDtypeStruct(arrived.shape, arrived.dtype)
    restored = call(emit_kernel, shape, (arrived,), 2**20)
    args[1], restored = lax.optimization_barrier((args[1], restored))
    turn_kv = call(
        turn_kernel,
        jax.ShapeDtypeStruct((count, HD), jnp.bfloat16),
        (t_own, t_code, *args, bias, t_tables),
        2**20,
    )
    return (restored.reshape(groups * BLK, HD), turn_kv)


def solution(mesh):
    placed = (
        P("pool", "mp"),
        P("pool"),
        P("pool"),
        P("pool"),
        P("pool", "mp"),
        P("pool"),
        P(None, "mp"),
        P("mp"),
    )
    return jax.shard_map(
        shards,
        mesh=mesh,
        in_specs=placed,
        out_specs=(P("pool", "mp"), P("pool", "mp")),
        check_vma=False,
    )
```

```python
import functools

import jax
import jax.numpy as jnp
from jax import lax
from jax.experimental import pallas as pl
from jax.experimental.pallas import tpu as pltpu
from jax.sharding import PartitionSpec as P

D = 8192
HD = 128
BLK = 64
KVD = 1024
NZ = 2
NX = 4
NC = 2
NY = 4
LIFT = 16384.0
STEPS = 2048.0
LN2 = 0.6931471805599453
LOW = 1e-36
HIGH = 3.39e38
FULL = 3.385e38
MOST = 6e4


def spot(z, x, c):
    return (z * NX + x) * NC + c


def pairs(move):
    return [
        (spot(z, x, c), spot(*move(z, x, c)))
        for z in range(NZ)
        for x in range(NX)
        for c in range(NC)
    ]


def across(v, e):
    return lax.ppermute(v, "mp", pairs(lambda z, x, c: (z ^ (e // NC), x, c ^ (e % NC))))


def outward(v, groups):
    ring = groups // NY
    moves = []
    for h in range(ring):
        for y in range(NY):
            for z, x, c in ((z, x, c) for z in range(NZ) for x in range(NX) for c in range(NC)):
                g = (h + 2 * z - 1) % ring * NY + y
                src = (h * NY + y) * NZ * NX * NC + spot(z, x, c)
                moves.append((src, g * NZ * NX * NC + spot(1 - z, x, 1 - c)))
    return lax.ppermute(v, ("pool", "mp"), moves)


def along_x(v, d):
    return lax.ppermute(v, "mp", pairs(lambda z, x, c: (z, (x + d) % NX, c)))


VMEM = pl.BlockSpec(memory_space=pltpu.VMEM)
SMEM = pl.BlockSpec(memory_space=pltpu.SMEM)
ANY = pl.BlockSpec(memory_space=pl.ANY)
f32 = jnp.float32


def diagonal():
    shape = (HD, HD)
    return lax.broadcasted_iota(jnp.int32, shape, 0) == lax.broadcasted_iota(jnp.int32, shape, 1)


def place():
    me = lax.axis_index("mp")
    return me // (NC * NX), lax.rem(me // NC, NX), lax.rem(me, NC)


def slice_kernel(w, w1, w2, w3, sems):
    z, _, c = place()
    copies = []
    for e, out in ((2, w2), (3, w3), (1, w1)):
        for k in range(NX):
            src = w.at[lax.bitwise_xor(z, e // NC), k, lax.bitwise_xor(c, e % NC)]
            copies.append(pltpu.make_async_copy(src, out.at[k], sems.at[len(copies)]))
    for copy in copies:
        copy.start()
    for copy in copies:
        copy.wait()


def slices(w):
    part = jax.ShapeDtypeStruct((NX,) + w.shape[3:], w.dtype)
    return pl.pallas_call(
        slice_kernel,
        out_shape=(part,) * 3,
        in_specs=[pl.BlockSpec(memory_space=pl.ANY)],
        out_specs=(VMEM,) * 3,
        scratch_shapes=[pltpu.SemaphoreType.DMA((3 * NX,))],
        cost_estimate=pl.CostEstimate(flops=0, bytes_accessed=2**21, transcendentals=0),
    )(w)


def anchor_kernel(x, after, out):
    out[...] = x[...]


def anchor(x, after):
    return pl.pallas_call(
        anchor_kernel,
        out_shape=jax.ShapeDtypeStruct(x.shape, x.dtype),
        in_specs=[VMEM, pl.BlockSpec(memory_space=pl.ANY)],
        out_specs=VMEM,
        compiler_params=pltpu.CompilerParams(vmem_limit_bytes=2**20),
        cost_estimate=pl.CostEstimate(flops=10**11, bytes_accessed=3 * 10**8, transcendentals=0),
    )(x, after)


def product(piece, j, weights, w0):
    _, x, _ = place()
    k = lax.rem(x - j + NX, NX)
    both = jnp.concatenate([w0[j]] + [w[k] for w in weights], axis=1)
    return jnp.dot(piece, both, preferred_element_type=f32)


def squared(piece):
    wide = piece.astype(f32)
    wide = wide * wide
    return sum(wide[:, g * HD : (g + 1) * HD] for g in range(wide.shape[1] // HD))


def fetch(w, w0, sems, order):
    z, x, c = place()
    copies = {}
    for j in order:
        src = w.at[z, lax.rem(x - j + NX, NX), c]
        copies[j] = pltpu.make_async_copy(src, w0.at[j], sems.at[j])
        copies[j].start()
    return copies


def first_kernel(w, r0, r1, r3, w1, w2, w3, acc, sq, w0, sems):
    rows = {0: r0, 1: r1, 3: r3}
    copies = fetch(w, w0, sems, rows)
    for j, r in rows.items():
        copies[j].wait()
        if j == 0:
            acc[...] = product(r[...], j, (w1, w2, w3), w0)
            sq[...] = squared(r[...])
        else:
            acc[...] += product(r[...], j, (w1, w2, w3), w0)
            sq[...] += squared(r[...])


def last_kernel(count, w, *refs):
    pieces, refs = refs[:count], refs[count:]
    w1, w2, w3, acc, sq, own, f1, f2, f3, code, w0, sems = refs
    fetch(w, w0, sems, (2,))[2].wait()
    piece = jnp.concatenate([r[...] for r in pieces], axis=0)
    total = acc[...] + product(piece, 2, (w1, w2, w3), w0)
    pack(total, sq[...] + squared(piece), own, f1, f2, f3, code)


def whole_kernel(w, r0, r1, r2, r3, w1, w2, w3, own, f1, f2, f3, code, w0, sems, rv, rs):
    order = (0, 1, 3, 2)
    moves = {}
    for j, r in enumerate((r0, r1, r2, r3)):
        moves[j] = pltpu.make_async_copy(r, rv.at[j], rs.at[j])
    moves[0].start()
    copies = fetch(w, w0, sems, order)
    for j in order[1:]:
        moves[j].start()
    total = sq = 0.0
    for j in order:
        copies[j].wait()
        moves[j].wait()
        total += product(rv[j], j, (w1, w2, w3), w0)
        sq += squared(rv[j])
    pack(total, sq, own, f1, f2, f3, code)


def pack(total, sq, own, f1, f2, f3, code):
    rows = own.shape[0]
    mask = diagonal()
    norm = jnp.clip(jnp.sum(sq, axis=1, keepdims=True), LOW, HIGH)
    down = LIFT * lax.rsqrt(norm)
    own[...] = total[:, :HD]
    for e, f in enumerate((f1, f2, f3)):
        sent = total[:, (e + 1) * HD : (e + 2) * HD] * down
        f[pl.ds(0, rows), :] = jnp.clip(sent, -MOST, MOST)
    lines = []
    for g in range(rows // HD):
        part = jnp.where(mask, norm[g * HD : (g + 1) * HD, :], 0.0)
        lines.append(jnp.sum(part, axis=0, keepdims=True))
    u = jnp.log(jnp.concatenate(lines, axis=0)) * (1.0 / LN2)
    whole = jnp.floor(u)
    part = (u - whole) * STEPS
    middle = jnp.floor(part)
    told = jnp.concatenate([whole, middle, part - middle, jnp.zeros_like(u)], axis=0)
    code[...] = told
    for f in (f1, f2, f3):
        f[pl.ds(rows, 16), :] = told


def multiply(body, rows, w, weights, held, out, grant, cost):
    stay = body is not whole_kernel
    moved = [pltpu.VMEM((NX,) + rows[0].shape, w.dtype), pltpu.SemaphoreType.DMA((NX,))]
    return pl.pallas_call(
        body,
        out_shape=out,
        in_specs=[ANY] + [VMEM if stay else ANY] * len(rows) + [VMEM] * (3 + len(held)),
        out_specs=(VMEM,) * len(out),
        scratch_shapes=[
            pltpu.VMEM((NX,) + w.shape[3:], w.dtype),
            pltpu.SemaphoreType.DMA((NX,)),
        ]
        + ([] if stay else moved),
        compiler_params=pltpu.CompilerParams(vmem_limit_bytes=grant * 2**20),
        cost_estimate=pl.CostEstimate(flops=cost * 2**30, bytes_accessed=2**22, transcendentals=0),
    )(w, *rows, *weights, *held)


def outputs(count):
    sent = jax.ShapeDtypeStruct((count + 16, HD), f32)
    return (
        jax.ShapeDtypeStruct((count, HD), f32),
        sent,
        sent,
        sent,
        jax.ShapeDtypeStruct((16, HD), f32),
    )


def half_width(parts):
    own, f1, f2, f3, code = parts
    return own, code, [f.astype(jnp.float16) for f in (f1, f2, f3)]


def call(body, out, args, flops, scalars=0):
    return pl.pallas_call(
        body,
        out_shape=out,
        in_specs=[SMEM] * scalars + [VMEM] * (len(args) - scalars),
        out_specs=jax.tree.map(lambda _: VMEM, out),
        compiler_params=pltpu.CompilerParams(vmem_limit_bytes=12 * 2**20),
        cost_estimate=pl.CostEstimate(flops=flops, bytes_accessed=2**20, transcendentals=0),
    )(*args)


def columns(own, code, got):
    lines = own.shape[0] // HD

    def norms_of(ref, first):
        u = ref[first : first + lines, :] + (
            ref[first + lines : first + 2 * lines, :]
            + ref[first + 2 * lines : first + 3 * lines, :]
        ) * (1.0 / STEPS)
        return jnp.exp(u * LN2)

    norms = [norms_of(g, own.shape[0]) for g in got]
    own_norm = norms_of(code, 0)
    total = own_norm + norms[0] + norms[1] + norms[2]
    for n in (own_norm, *norms):
        total = jnp.where(n > FULL, jnp.inf, total)
    scale = lax.rsqrt(total / D + 1e-06)
    ups = [jnp.sqrt(n) * scale * (1.0 / LIFT) for n in norms]
    rest = jnp.zeros((HD - 4 * lines, HD), f32)
    return jnp.concatenate([scale, *ups, rest], axis=0).T


def finished(k, cols, own, got, bias, turns):
    at = slice(k * HD, (k + 1) * HD)
    lines = own.shape[0] // HD
    value = own[at, :] * cols[:, k : k + 1] + bias[...]
    for d, g in enumerate(got):
        j = (d + 1) * lines + k
        value += g[at, :] * cols[:, j : j + 1]
    turn = turns[at, :]
    swapped = pltpu.roll(turn, HD // 2, 1)
    first = lax.broadcasted_iota(jnp.int32, turn.shape, 1) < HD // 2
    cosine = jnp.where(first, turn, swapped)
    sine = jnp.where(first, -swapped, turn)
    return value * cosine + pltpu.roll(value, HD // 2, 1) * sine


def emit_kernel(arrived, cache):
    cache[...] = arrived[...]


def turn_kernel(own, code, g1, g2, g3, bias, turns, out):
    cols = columns(own, code, (g1, g2, g3))
    for k in range(own.shape[0] // HD):
        value = finished(k, cols, own, (g1, g2, g3), bias, turns)
        out[k * HD : (k + 1) * HD, :] = value.astype(out.dtype)


def stored_kernel(owner, valid, own, code, g1, g2, g3, bias, turns, out):
    row = lax.broadcasted_iota(jnp.int32, (BLK, HD), 0)
    out[...] = jnp.zeros(out.shape, out.dtype)
    cols = columns(own, code, (g1, g2, g3))
    for k in range(own.shape[0] // HD):
        value = finished(k, cols, own, (g1, g2, g3), bias, turns)
        for h in range(HD // BLK):
            b = k * (HD // BLK) + h
            kept = jnp.where(row < valid[b], value[h * BLK : (h + 1) * BLK], 0.0)
            out[owner[b]] = kept.astype(out.dtype)


def tables(positions, is_key):
    half = HD // 2
    freq = jnp.exp(
        -jnp.log(jnp.float32(1000000.0)) * (jnp.arange(half).astype(jnp.float32) * 2.0 / HD)
    )
    angle = positions.astype(jnp.float32)[:, None] * jnp.concatenate([freq, freq])[None, :]
    first = (jnp.arange(HD) < half)[None, :]
    plain = jnp.where(first, 1.0, 0.0)
    return jnp.where(is_key, jnp.where(first, jnp.cos(angle), jnp.sin(angle)), plain)


def shards(
    stored_hidden,
    block_owner,
    block_valid,
    block_start,
    turn_hidden,
    turn_position,
    kv_weight,
    kv_bias,
):
    groups = lax.axis_size("pool")
    me = lax.axis_index("mp")
    is_key = me * HD < KVD
    count, local = stored_hidden.shape
    bias = kv_bias[None, :]

    chunks = kv_weight.reshape(NZ, NX, NC, local, HD)

    positions = (block_start[:, None] + jnp.arange(BLK)[None, :]).reshape(-1)
    s_tables = tables(positions, is_key)
    t_tables = tables(turn_position, is_key)

    s1 = along_x(stored_hidden, 1)
    s3 = along_x(stored_hidden, 3)
    parts = slices(chunks)
    held = anchor(bias, parts[0])
    w1, w2, w3 = parts
    w2 = across(w2, 2)
    w3 = outward(w3, groups)
    w1, _ = lax.optimization_barrier((w1, s3))
    w1 = across(w1, 1)
    weights = [w1, w2, w3]
    half = count // 2
    s1, s_tables, t_tables = lax.optimization_barrier((s1, s_tables, t_tables))
    s2a = along_x(s1[:half], 1)
    s2b = along_x(s3[half:], 3)
    row, s1, s3, bias = lax.optimization_barrier((turn_hidden, s1, s3, held))
    t1 = along_x(row, 1)
    t3 = along_x(row, 3)
    partly = (
        jax.ShapeDtypeStruct((count, 4 * HD), f32),
        jax.ShapeDtypeStruct((count, HD), f32),
    )
    acc, sq = multiply(first_kernel, (stored_hidden, s1, s3), chunks, weights, (), partly, 16,1)
    row, acc = lax.optimization_barrier((turn_hidden, acc))
    t2 = along_x(row, 2)
    last = functools.partial(last_kernel, 2)
    parts = multiply(last, (s2a, s2b), chunks, weights, (acc, sq), outputs(count), 16,1)
    s_own, s_code, s_sent = half_width(parts)
    s_g1, s_g2, s_g3 = [across(v, e) for e, v in zip((1, 2, 3), s_sent)]
    t_rows = [turn_hidden, t1, t2, t3]

    args = [v.astype(f32) for v in (s_g1, s_g2, s_g3)]
    outgoing = call(
        stored_kernel,
        jax.ShapeDtypeStruct((groups, BLK, HD), jnp.bfloat16),
        (block_owner, block_valid, s_own, s_code, *args, bias, s_tables),
        2**20,
        2,
    )
    arrived = lax.all_to_all(outgoing, "pool", split_axis=0, concat_axis=0, tiled=True)

    t_rows[0], outgoing = lax.optimization_barrier((t_rows[0], outgoing))
    parts = multiply(whole_kernel, t_rows, chunks, weights, (), outputs(count), 16,2)
    t_own, t_code, t_sent = half_width(parts)
    t1, t2, t3 = t_sent
    t_got = across(t1, 1), across(t2, 2), across(t3, 3)
    args = [v.astype(f32) for v in t_got]
    shape = jax.ShapeDtypeStruct(arrived.shape, arrived.dtype)
    restored = call(emit_kernel, shape, (arrived,), 2**20)
    args[1], restored = lax.optimization_barrier((args[1], restored))
    turn_kv = call(
        turn_kernel,
        jax.ShapeDtypeStruct((count, HD), jnp.bfloat16),
        (t_own, t_code, *args, bias, t_tables),
        2**20,
    )
    return (restored.reshape(groups * BLK, HD), turn_kv)


def solution(mesh):
    placed = (
        P("pool", "mp"),
        P("pool"),
        P("pool"),
        P("pool"),
        P("pool", "mp"),
        P("pool"),
        P(None, "mp"),
        P("mp"),
    )
    return jax.shard_map(
        shards,
        mesh=mesh,
        in_specs=placed,
        out_specs=(P("pool", "mp"), P("pool", "mp")),
        check_vma=False,
    )
```

```python
import functools

import jax
import jax.numpy as jnp
from jax import lax
from jax.experimental import pallas as pl
from jax.experimental.pallas import tpu as pltpu
from jax.sharding import PartitionSpec as P

D = 8192
HD = 128
BLK = 64
KVD = 1024
NZ = 2
NX = 4
NC = 2
NY = 4
LIFT = 16384.0
STEPS = 2048.0
LN2 = 0.6931471805599453
LOW = 1e-36
HIGH = 3.39e38
FULL = 3.385e38
MOST = 6e4


def spot(z, x, c):
    return (z * NX + x) * NC + c


def pairs(move):
    return [
        (spot(z, x, c), spot(*move(z, x, c)))
        for z in range(NZ)
        for x in range(NX)
        for c in range(NC)
    ]


def across(v, e):
    return lax.ppermute(v, "mp", pairs(lambda z, x, c: (z ^ (e // NC), x, c ^ (e % NC))))


def outward(v, groups):
    ring = groups // NY
    moves = []
    for h in range(ring):
        for y in range(NY):
            for z, x, c in ((z, x, c) for z in range(NZ) for x in range(NX) for c in range(NC)):
                g = (h + 2 * z - 1) % ring * NY + y
                src = (h * NY + y) * NZ * NX * NC + spot(z, x, c)
                moves.append((src, g * NZ * NX * NC + spot(1 - z, x, 1 - c)))
    return lax.ppermute(v, ("pool", "mp"), moves)


def along_x(v, d):
    return lax.ppermute(v, "mp", pairs(lambda z, x, c: (z, (x + d) % NX, c)))


VMEM = pl.BlockSpec(memory_space=pltpu.VMEM)
SMEM = pl.BlockSpec(memory_space=pltpu.SMEM)
ANY = pl.BlockSpec(memory_space=pl.ANY)
f32 = jnp.float32


def diagonal():
    shape = (HD, HD)
    return lax.broadcasted_iota(jnp.int32, shape, 0) == lax.broadcasted_iota(jnp.int32, shape, 1)


def place():
    me = lax.axis_index("mp")
    return me // (NC * NX), lax.rem(me // NC, NX), lax.rem(me, NC)


def slice_kernel(which, w, *refs):
    z, _, c = place()
    outs, held, sems = refs[: len(which)], refs[-2], refs[-1]
    into, away = [], []
    for n, (e, out) in enumerate(zip(which, outs)):
        for k in range(NX):
            src = w.at[lax.bitwise_xor(z, e // NC), k, lax.bitwise_xor(c, e % NC)]
            at = n * NX + k
            into.append(pltpu.make_async_copy(src, held.at[at], sems.at[0, at]))
            away.append(pltpu.make_async_copy(held.at[at], out.at[k], sems.at[1, at]))
    for copy in into:
        copy.start()
    for copy, leave in zip(into, away):
        copy.wait()
        leave.start()
    for leave in away:
        leave.wait()


def slices(w, which):
    part = jax.ShapeDtypeStruct((NX,) + w.shape[3:], w.dtype)
    count = NX * len(which)
    return pl.pallas_call(
        functools.partial(slice_kernel, which),
        out_shape=(part,) * len(which),
        in_specs=[ANY],
        out_specs=(ANY,) * len(which),
        scratch_shapes=[
            pltpu.VMEM((count,) + w.shape[3:], w.dtype),
            pltpu.SemaphoreType.DMA((2, count)),
        ],
        cost_estimate=pl.CostEstimate(flops=0, bytes_accessed=2**21, transcendentals=0),
    )(w)


def anchor_kernel(x, after, out):
    out[...] = x[...]


def anchor(x, after):
    return pl.pallas_call(
        anchor_kernel,
        out_shape=jax.ShapeDtypeStruct(x.shape, x.dtype),
        in_specs=[VMEM, pl.BlockSpec(memory_space=pl.ANY)],
        out_specs=VMEM,
        compiler_params=pltpu.CompilerParams(vmem_limit_bytes=2**20),
        cost_estimate=pl.CostEstimate(flops=10**11, bytes_accessed=3 * 10**8, transcendentals=0),
    )(x, after)


def product(piece, j, weights, w0):
    _, x, _ = place()
    k = lax.rem(x - j + NX, NX)
    both = jnp.concatenate([w0[j]] + [w[k] for w in weights], axis=1)
    return jnp.dot(piece, both, preferred_element_type=f32)


def squared(piece):
    wide = piece.astype(f32)
    wide = wide * wide
    return sum(wide[:, g * HD : (g + 1) * HD] for g in range(wide.shape[1] // HD))


def fetch(w, w0, sems, order):
    z, x, c = place()
    copies = {}
    for j in order:
        src = w.at[z, lax.rem(x - j + NX, NX), c]
        copies[j] = pltpu.make_async_copy(src, w0.at[j], sems.at[j])
        copies[j].start()
    return copies


def first_kernel(w, r0, r1, r3, w1, w2, w3, acc, sq, w0, sems):
    rows = {0: r0, 1: r1, 3: r3}
    copies = fetch(w, w0, sems, rows)
    for j, r in rows.items():
        copies[j].wait()
        if j == 0:
            acc[...] = product(r[...], j, (w1, w2, w3), w0)
            sq[...] = squared(r[...])
        else:
            acc[...] += product(r[...], j, (w1, w2, w3), w0)
            sq[...] += squared(r[...])


def last_kernel(count, w, *refs):
    pieces, refs = refs[:count], refs[count:]
    w1, w2, w3, acc, sq, own, f1, f2, f3, code, w0, sems = refs
    fetch(w, w0, sems, (2,))[2].wait()
    piece = jnp.concatenate([r[...] for r in pieces], axis=0)
    total = acc[...] + product(piece, 2, (w1, w2, w3), w0)
    pack(total, sq[...] + squared(piece), own, f1, f2, f3, code)


def whole_kernel(w, r0, r1, r2, r3, w1, w2, w3, own, f1, f2, f3, code, w0, sems, rv, rs):
    order = (0, 1, 3, 2)
    moves = {}
    for j, r in enumerate((r0, r1, r2, r3)):
        moves[j] = pltpu.make_async_copy(r, rv.at[j], rs.at[j])
    moves[0].start()
    copies = fetch(w, w0, sems, order)
    for j in order[1:]:
        moves[j].start()
    total = sq = 0.0
    for j in order:
        copies[j].wait()
        moves[j].wait()
        total += product(rv[j], j, (w1, w2, w3), w0)
        sq += squared(rv[j])
    pack(total, sq, own, f1, f2, f3, code)


def pack(total, sq, own, f1, f2, f3, code):
    rows = own.shape[0]
    mask = diagonal()
    norm = jnp.clip(jnp.sum(sq, axis=1, keepdims=True), LOW, HIGH)
    down = LIFT * lax.rsqrt(norm)
    own[...] = total[:, :HD]
    for e, f in enumerate((f1, f2, f3)):
        sent = total[:, (e + 1) * HD : (e + 2) * HD] * down
        f[pl.ds(0, rows), :] = jnp.clip(sent, -MOST, MOST)
    lines = []
    for g in range(rows // HD):
        part = jnp.where(mask, norm[g * HD : (g + 1) * HD, :], 0.0)
        lines.append(jnp.sum(part, axis=0, keepdims=True))
    u = jnp.log(jnp.concatenate(lines, axis=0)) * (1.0 / LN2)
    whole = jnp.floor(u)
    part = (u - whole) * STEPS
    middle = jnp.floor(part)
    told = jnp.concatenate([whole, middle, part - middle, jnp.zeros_like(u)], axis=0)
    code[...] = told
    for f in (f1, f2, f3):
        f[pl.ds(rows, 16), :] = told


def multiply(body, rows, w, weights, held, out, grant, cost):
    stay = body is not whole_kernel
    moved = [pltpu.VMEM((NX,) + rows[0].shape, w.dtype), pltpu.SemaphoreType.DMA((NX,))]
    return pl.pallas_call(
        body,
        out_shape=out,
        in_specs=[ANY] + [VMEM if stay else ANY] * len(rows) + [VMEM] * (3 + len(held)),
        out_specs=(VMEM,) * len(out),
        scratch_shapes=[
            pltpu.VMEM((NX,) + w.shape[3:], w.dtype),
            pltpu.SemaphoreType.DMA((NX,)),
        ]
        + ([] if stay else moved),
        compiler_params=pltpu.CompilerParams(vmem_limit_bytes=grant * 2**20),
        cost_estimate=pl.CostEstimate(flops=cost * 2**30, bytes_accessed=2**22, transcendentals=0),
    )(w, *rows, *weights, *held)


def outputs(count):
    sent = jax.ShapeDtypeStruct((count + 16, HD), f32)
    return (
        jax.ShapeDtypeStruct((count, HD), f32),
        sent,
        sent,
        sent,
        jax.ShapeDtypeStruct((16, HD), f32),
    )


def half_width(parts):
    own, f1, f2, f3, code = parts
    return own, code, [f.astype(jnp.float16) for f in (f1, f2, f3)]


def call(body, out, args, flops, scalars=0):
    return pl.pallas_call(
        body,
        out_shape=out,
        in_specs=[SMEM] * scalars + [VMEM] * (len(args) - scalars),
        out_specs=jax.tree.map(lambda _: VMEM, out),
        compiler_params=pltpu.CompilerParams(vmem_limit_bytes=12 * 2**20),
        cost_estimate=pl.CostEstimate(flops=flops, bytes_accessed=2**20, transcendentals=0),
    )(*args)


def columns(own, code, got):
    lines = own.shape[0] // HD

    def norms_of(ref, first):
        u = ref[first : first + lines, :] + (
            ref[first + lines : first + 2 * lines, :]
            + ref[first + 2 * lines : first + 3 * lines, :]
        ) * (1.0 / STEPS)
        return jnp.exp(u * LN2)

    norms = [norms_of(g, own.shape[0]) for g in got]
    own_norm = norms_of(code, 0)
    total = own_norm + norms[0] + norms[1] + norms[2]
    for n in (own_norm, *norms):
        total = jnp.where(n > FULL, jnp.inf, total)
    scale = lax.rsqrt(total / D + 1e-06)
    ups = [jnp.sqrt(n) * scale * (1.0 / LIFT) for n in norms]
    rest = jnp.zeros((HD - 4 * lines, HD), f32)
    return jnp.concatenate([scale, *ups, rest], axis=0).T


def finished(k, cols, own, got, bias, turns):
    at = slice(k * HD, (k + 1) * HD)
    lines = own.shape[0] // HD
    value = own[at, :] * cols[:, k : k + 1] + bias[...]
    for d, g in enumerate(got):
        j = (d + 1) * lines + k
        value += g[at, :] * cols[:, j : j + 1]
    turn = turns[at, :]
    swapped = pltpu.roll(turn, HD // 2, 1)
    first = lax.broadcasted_iota(jnp.int32, turn.shape, 1) < HD // 2
    cosine = jnp.where(first, turn, swapped)
    sine = jnp.where(first, -swapped, turn)
    return value * cosine + pltpu.roll(value, HD // 2, 1) * sine


def emit_kernel(arrived, cache):
    cache[...] = arrived[...]


def turn_kernel(own, code, g1, g2, g3, bias, turns, out):
    cols = columns(own, code, (g1, g2, g3))
    for k in range(own.shape[0] // HD):
        value = finished(k, cols, own, (g1, g2, g3), bias, turns)
        out[k * HD : (k + 1) * HD, :] = value.astype(out.dtype)


def stored_kernel(owner, valid, own, code, g1, g2, g3, bias, turns, out):
    row = lax.broadcasted_iota(jnp.int32, (BLK, HD), 0)
    out[...] = jnp.zeros(out.shape, out.dtype)
    cols = columns(own, code, (g1, g2, g3))
    for k in range(own.shape[0] // HD):
        value = finished(k, cols, own, (g1, g2, g3), bias, turns)
        for h in range(HD // BLK):
            b = k * (HD // BLK) + h
            kept = jnp.where(row < valid[b], value[h * BLK : (h + 1) * BLK], 0.0)
            out[owner[b]] = kept.astype(out.dtype)


def tables(positions, is_key):
    half = HD // 2
    freq = jnp.exp(
        -jnp.log(jnp.float32(1000000.0)) * (jnp.arange(half).astype(jnp.float32) * 2.0 / HD)
    )
    angle = positions.astype(jnp.float32)[:, None] * jnp.concatenate([freq, freq])[None, :]
    first = (jnp.arange(HD) < half)[None, :]
    plain = jnp.where(first, 1.0, 0.0)
    return jnp.where(is_key, jnp.where(first, jnp.cos(angle), jnp.sin(angle)), plain)


def shards(
    stored_hidden,
    block_owner,
    block_valid,
    block_start,
    turn_hidden,
    turn_position,
    kv_weight,
    kv_bias,
):
    groups = lax.axis_size("pool")
    me = lax.axis_index("mp")
    is_key = me * HD < KVD
    count, local = stored_hidden.shape
    bias = kv_bias[None, :]

    chunks = kv_weight.reshape(NZ, NX, NC, local, HD)

    positions = (block_start[:, None] + jnp.arange(BLK)[None, :]).reshape(-1)
    s_tables = tables(positions, is_key)
    t_tables = tables(turn_position, is_key)

    s1 = along_x(stored_hidden, 1)
    s3 = along_x(stored_hidden, 3)
    w3, w2, w1 = slices(chunks, (3, 2, 1))
    held = anchor(bias, w3)
    w2 = across(w2, 2)
    w3 = outward(w3, groups)
    w1, _ = lax.optimization_barrier((w1, s3))
    w1 = across(w1, 1)
    weights = [w1, w2, w3]
    half = count // 2
    s1, s_tables, t_tables = lax.optimization_barrier((s1, s_tables, t_tables))
    s2a = along_x(s1[:half], 1)
    s2b = along_x(s3[half:], 3)
    row, s1, s3, bias = lax.optimization_barrier((turn_hidden, s1, s3, held))
    t1 = along_x(row, 1)
    t3 = along_x(row, 3)
    partly = (
        jax.ShapeDtypeStruct((count, 4 * HD), f32),
        jax.ShapeDtypeStruct((count, HD), f32),
    )
    acc, sq = multiply(first_kernel, (stored_hidden, s1, s3), chunks, weights, (), partly, 16,1)
    row, acc = lax.optimization_barrier((turn_hidden, acc))
    t2 = along_x(row, 2)
    last = functools.partial(last_kernel, 2)
    parts = multiply(last, (s2a, s2b), chunks, weights, (acc, sq), outputs(count), 16,1)
    s_own, s_code, s_sent = half_width(parts)
    s_g2, s_g3, s_g1 = [across(s_sent[e - 1], e) for e in (2, 3, 1)]
    t_rows = [turn_hidden, t1, t2, t3]

    args = [v.astype(f32) for v in (s_g1, s_g2, s_g3)]
    outgoing = call(
        stored_kernel,
        jax.ShapeDtypeStruct((groups, BLK, HD), jnp.bfloat16),
        (block_owner, block_valid, s_own, s_code, *args, bias, s_tables),
        2**20,
        2,
    )
    arrived = lax.all_to_all(outgoing, "pool", split_axis=0, concat_axis=0, tiled=True)

    t_rows[0], outgoing = lax.optimization_barrier((t_rows[0], outgoing))
    parts = multiply(whole_kernel, t_rows, chunks, weights, (), outputs(count), 16,2)
    t_own, t_code, t_sent = half_width(parts)
    t1, t2, t3 = t_sent
    t_g2, t_g3, t_g1 = across(t2, 2), across(t3, 3), across(t1, 1)
    t_got = t_g1, t_g2, t_g3
    args = [v.astype(f32) for v in t_got]
    shape = jax.ShapeDtypeStruct(arrived.shape, arrived.dtype)
    restored = call(emit_kernel, shape, (arrived,), 2**20)
    args[1], restored = lax.optimization_barrier((args[1], restored))
    turn_kv = call(
        turn_kernel,
        jax.ShapeDtypeStruct((count, HD), jnp.bfloat16),
        (t_own, t_code, *args, bias, t_tables),
        2**20,
    )
    return (restored.reshape(groups * BLK, HD), turn_kv)


def solution(mesh):
    placed = (
        P("pool", "mp"),
        P("pool"),
        P("pool"),
        P("pool"),
        P("pool", "mp"),
        P("pool"),
        P(None, "mp"),
        P("mp"),
    )
    return jax.shard_map(
        shards,
        mesh=mesh,
        in_specs=placed,
        out_specs=(P("pool", "mp"), P("pool", "mp")),
        check_vma=False,
    )
```
